32 devices in a mesh: ax: 16 (over z, x, core), rad: 2 (over y).
Axes of the slice: x: 2, y: 2, z: 4, core: 2. Of those that a mesh axis runs over, the one named last changes fastest.
Arguments:
- field: float32 [4, 256, 128, 256], P(None, 'ax', 'rad'), may hold values from -75 to 75
- start_az: float32 [256, 32], replicated, may hold values from -6 to 6
- start_rad: float32 [128, 32], replicated, may hold values from -6 to 6
Outputs:
- core: float32 [4, 256, 1024], P(None, 'ax', 'rad')
- az_factor: float32 [256, 32], replicated
- rad_factor: float32 [128, 32], replicated
The draws below stay inside these ranges and needn't reach their ends.
All inputs are finite; a program needn't handle non-finite values.
Results may differ from the reference program's by a relative error of at most 0.0003.
Values sent between devices are 32-bit elements; how exact they have to be, the bound alone decides.
A program may use at most 128 MiB of HBM per device.

```python
import jax
import jax.numpy as jnp
from jax import lax

NS = 4
NT = 256
RANK = 32
ITERS = 3
NA = 256
NR = 128


def draw_field(key, part):
    key = jax.random.fold_in(key, 1)
    keys = jax.random.split(key, 8)
    modes = 48
    shape = (NS, NA, NR, NT)
    coef = jnp.clip(jax.random.normal(keys[0], (NS, NA, modes), jnp.float32), -4.0, 4.0)
    noise = 0.45 * jnp.clip(jax.random.normal(keys[1], shape, jnp.float32), -6.0, 6.0)
    spread = 0.7
    decay = 0.35
    weights = (1.0 + jnp.arange(modes, dtype=jnp.float32)) ** (-decay)
    coef = coef * weights[None, None, :]
    az_wave = jax.random.randint(keys[2], (modes,), 1, NT // 2 + 1).astype(jnp.float32)
    rad_wave = jax.random.randint(keys[3], (modes,), 0, NR // 2 + 1).astype(jnp.float32)
    az_phase = jax.random.uniform(keys[4], (modes,), jnp.float32, -jnp.pi, jnp.pi)
    rad_phase = jax.random.uniform(keys[5], (modes,), jnp.float32, -jnp.pi, jnp.pi)
    cells_t = jnp.arange(NT, dtype=jnp.float32)
    cells_r = jnp.arange(NR, dtype=jnp.float32) + 0.5
    az_prof = jnp.cos(2.0 * jnp.pi * az_wave[:, None] * cells_t[None, :] / NT + az_phase[:, None])
    rad_prof = jnp.cos(jnp.pi * rad_wave[:, None] * cells_r[None, :] / NR + rad_phase[:, None])

    def add_mode(index, total):
        weight_sa = lax.dynamic_index_in_dim(coef, index, 2, keepdims=False)
        profile_r = lax.dynamic_index_in_dim(rad_prof, index, 0, keepdims=False)
        profile_t = lax.dynamic_index_in_dim(az_prof, index, 0, keepdims=False)
        return total + weight_sa[:, :, None, None] * profile_r[None, None, :, None] * profile_t[None, None, None, :]
    modal = lax.fori_loop(0, modes, add_mode, jnp.zeros(shape, jnp.float32))
    rough_rad = jnp.exp(jax.random.uniform(keys[6], (NR,), jnp.float32, -spread, spread))
    rough_az = jnp.exp(jax.random.uniform(keys[7], (NT,), jnp.float32, -spread, spread))
    amplitude = 1.0 + 2.0 * jnp.arange(NA, dtype=jnp.float32) / max(NA - 1, 1)
    values = (modal + noise) * amplitude[None, :, None, None] * rough_rad[None, None, :, None] * rough_az[None, None, None, :]
    return jnp.clip(values, -75.0, 75.0)


def scatter_about(own_key, extent, width, reach, kind=jnp.bfloat16):
    drawn = width * jax.random.normal(own_key, extent, jnp.float32)
    return jnp.clip(drawn, min=-reach, max=reach).astype(kind)


def setup_inputs(seed: int = 0) -> dict:
    arg_keys = jax.random.split(jax.random.key(seed), 4)
    return {
        "field": draw_field(jax.random.fold_in(arg_keys[3], 71), 0),
        "start_az": scatter_about(arg_keys[1], (NT, RANK), 1.0, 6.0, jnp.float32),
        "start_rad": scatter_about(arg_keys[2], (NR, RANK), 1.0, 6.0, jnp.float32),
    }


HIGH = lax.Precision.HIGHEST

def orthonormal(block):
    inner = jnp.dot(block.T.astype(jnp.float32), block.astype(jnp.float32), precision=HIGH, preferred_element_type=jnp.float32)
    lower = jnp.linalg.cholesky(inner)
    return lax.linalg.triangular_solve(lower, block, left_side=False, lower=True, transpose_a=True)

def reference(field, start_az, start_rad):
    flat = field.reshape(-1, NT)
    gram_az = jnp.dot(flat.T.astype(jnp.float32), flat.astype(jnp.float32), precision=HIGH, preferred_element_type=jnp.float32)
    az_factor = start_az
    for step in range(ITERS):
        az_factor = orthonormal(jnp.dot(gram_az.astype(jnp.float32), az_factor.astype(jnp.float32), precision=HIGH, preferred_element_type=jnp.float32))
    proj = jnp.dot(flat.astype(jnp.float32), az_factor.astype(jnp.float32), precision=HIGH, preferred_element_type=jnp.float32).reshape(NS, NA, NR, RANK)
    gram_rad = jnp.einsum('sark,saqk->rq', proj, proj, precision=HIGH)
    rad_factor = start_rad
    for step in range(ITERS):
        rad_factor = orthonormal(jnp.dot(gram_rad.astype(jnp.float32), rad_factor.astype(jnp.float32), precision=HIGH, preferred_element_type=jnp.float32))
    core = jnp.einsum('sark,rj->sakj', proj, rad_factor, precision=HIGH).reshape(NS, NA, RANK * RANK)
    return (core, az_factor, rad_factor)
```

```python
import functools

import jax
import jax.numpy as jnp
from jax import lax
from jax.experimental import pallas as pl
from jax.experimental.pallas import tpu as pltpu
from jax.sharding import PartitionSpec as P

ITERS = 3
LANES = 128
PANEL = 8
HIGH = lax.Precision.HIGHEST
MESH = pl.DeviceIdType.MESH
F32 = jnp.float32
BF16 = jnp.bfloat16
VMEM_LIMIT = 48 * 1024 * 1024


def dot(a, b, ca, cb, precision=HIGH):
    return lax.dot_general(
        a, b, (((ca,), (cb,)), ((), ())), precision=precision, preferred_element_type=F32
    )


def dot16(a, b, ca, cb):
    return dot(a, b, ca, cb, lax.Precision.DEFAULT)


def split(value):
    high = value.astype(BF16)
    return high, (value - high.astype(F32)).astype(BF16)


class Groups:
    def __init__(self, n_ax, n_rad, low):
        self.low = min(low, n_ax)
        self.n_rad = n_rad
        self.near = self.low * n_rad
        self.far = n_ax // self.low

    def place(self):
        ax, rad = lax.axis_index("ax"), lax.axis_index("rad")
        return lax.rem(ax, self.low) * self.n_rad + rad, lax.div(ax, self.low)

    def device(self, near, far):
        return (far * self.low + lax.div(near, self.n_rad), lax.rem(near, self.n_rad))

    def rows(self, total):
        return -(-total // (self.near * 8)) * 8

    def greet(self):
        near, far = self.place()
        barrier = pltpu.get_barrier_semaphore()
        for step in range(1, self.near):
            peer = lax.rem(near + step, self.near)
            pl.semaphore_signal(barrier, inc=1, device_id=self.device(peer, far), device_id_type=MESH)
        for step in range(1, self.far):
            peer = lax.rem(far + step, self.far)
            pl.semaphore_signal(barrier, inc=1, device_id=self.device(near, peer), device_id_type=MESH)

    def meet(self):
        pl.semaphore_wait(pltpu.get_barrier_semaphore(), self.near + self.far - 2)

    def scratch(self, rows):
        return [
            pltpu.VMEM((self.near, rows, LANES), F32),
            pltpu.VMEM((self.far, rows, LANES), F32),
            pltpu.SemaphoreType.DMA((2, self.near)),
            pltpu.SemaphoreType.DMA((2, self.far)),
            pltpu.SemaphoreType.DMA((2, self.near)),
        ]

    def all_sum(self, rows, part, out, terms, pieces, sem_a, sem_b, sem_c):
        near, far = self.place()

        def mine(index):
            return pl.ds(pl.multiple_of(index * rows, 8), rows)

        sent = []
        for step in range(1, self.near):
            peer = lax.rem(near + step, self.near)
            sent.append(pltpu.make_async_remote_copy(
                src_ref=part.at[mine(peer)], dst_ref=terms.at[step],
                send_sem=sem_a.at[0, step], recv_sem=sem_a.at[1, step],
                device_id=self.device(peer, far), device_id_type=MESH))
            sent[-1].start()
        total = part[mine(near), :]
        for step in range(1, self.near):
            sent[step - 1].wait_recv()
            total = total + terms[step]
        pieces[far] = total
        for step in range(1, self.far):
            peer = lax.rem(far + step, self.far)
            sent.append(pltpu.make_async_remote_copy(
                src_ref=pieces.at[far], dst_ref=pieces.at[far],
                send_sem=sem_b.at[0, step], recv_sem=sem_b.at[1, step],
                device_id=self.device(near, peer), device_id_type=MESH))
            sent[-1].start()
        for copy in sent[self.near - 1:]:
            copy.wait_recv()
        total = pieces[0]
        for index in range(1, self.far):
            total = total + pieces[index]
        out[mine(near), :] = total
        last = []
        for step in range(1, self.near):
            peer = lax.rem(near + step, self.near)
            last.append(pltpu.make_async_remote_copy(
                src_ref=out.at[mine(near)], dst_ref=out.at[mine(near)],
                send_sem=sem_c.at[0, step], recv_sem=sem_c.at[1, step],
                device_id=self.device(peer, far), device_id_type=MESH))
            last[-1].start()
        for copy in last:
            copy.wait_recv()
        for copy in sent + last:
            copy.wait_send()


def gram_az_kernel(groups, rows, chunk, field, out, part, *scratch):
    groups.greet()
    count, azim = field.shape
    half = azim // 2

    def add(step, totals):
        cells = field[pl.ds(pl.multiple_of(step * chunk, chunk), chunk), :]
        high, low = split(cells)
        return (
            totals[0] + dot16(high, high, 0, 0) + dot16(low, low, 0, 0),
            totals[1] + dot16(high, low, 0, 0),
        )

    zero = jnp.zeros((azim, azim), F32)
    even, mixed = lax.fori_loop(0, count // chunk, add, (zero, zero))
    gram = even + mixed + mixed.T
    part[0:half] = gram[:half, :half]
    part[half:2 * half] = gram[:half, half:]
    part[2 * half:3 * half] = gram[half:, half:]
    if part.shape[0] > 3 * half:
        part[3 * half:] = jnp.zeros((part.shape[0] - 3 * half, LANES), F32)
    groups.meet()
    groups.all_sum(rows, part, out, *scratch)


def orthonormal(block):
    rank = block.shape[0]
    inner = dot(block, block, 1, 1)
    index = lax.broadcasted_iota(jnp.int32, (rank, LANES), 0)
    done = []
    for start in range(0, rank, PANEL):
        columns = [
            jnp.broadcast_to(inner[:, start + i:start + i + 1], (rank, LANES)) for i in range(PANEL)
        ]
        for i in range(PANEL):
            k = start + i
            pivot = columns[i][k:k + 1, :]
            inv = lax.rsqrt(pivot)
            inv = inv * (1.5 - 0.5 * pivot * inv * inv)
            lower = jnp.where(index > k, columns[i] * inv, 0.0)
            for j in range(i + 1, PANEL):
                columns[j] = columns[j] - lower * lower[start + j:start + j + 1, :]
            wide = jnp.concatenate([inv] * (block.shape[1] // LANES), axis=1)
            row = block[k:k + 1, :] * wide
            done.append(row)
            spread = jnp.concatenate([lower] * (block.shape[1] // LANES), axis=1)
            block = block - spread * row
            inner = inner - lower[:, :rank] * (inner[k:k + 1, :] * inv[:, :rank])
    return jnp.concatenate(done, axis=0)


def iterate(gram, start):
    block = orthonormal(dot(start, gram, 0, 0))
    for _ in range(ITERS - 1):
        block = orthonormal(dot(block, gram, 1, 0))
    return block


def az_kernel(group, field, packed, start, factor, proj):
    cells, radial, azim = field.shape
    rank = start.shape[1]
    half = azim // 2
    width = LANES // radial
    pairs = cells // width
    cross = packed[half:2 * half, :]
    gram = jnp.concatenate([
        jnp.concatenate([packed[0:half, :], cross], axis=1),
        jnp.concatenate([cross.T, packed[2 * half:3 * half, :]], axis=1),
    ], axis=0)
    block = iterate(gram, start[...])
    factor[...] = block.T
    high, low = split(block)
    both = jnp.concatenate([high, low], axis=0)

    def project(step, carry):
        first = step * group
        part = jnp.concatenate(
            [field[pl.ds(e * pairs + first, group)] for e in range(width)], axis=1
        ).reshape(group * LANES, azim)
        f_high, f_low = split(part)
        twice = dot16(both, f_high, 1, 1)
        values = twice[:rank] + twice[rank:] + dot16(high, f_low, 1, 1)
        block = jnp.stack([values[:, i * LANES:(i + 1) * LANES] for i in range(group)], axis=1)
        proj[:, pl.ds(pl.multiple_of(first, 8), group), :] = block
        return carry

    lax.fori_loop(0, pairs // group, project, 0)


def gram_rad_kernel(groups, rows, radial, proj, out, held, part, sems, local_sem, *scratch):
    groups.greet()
    n_rad, local_rank, pairs, _ = proj.shape
    ax, me = lax.axis_index("ax"), lax.axis_index("rad")
    own = pltpu.make_async_copy(proj.at[me], held.at[me], local_sem)
    own.start()
    groups.meet()
    copies = []
    for step in range(1, n_rad):
        peer = lax.rem(me + step, n_rad)
        copies.append(pltpu.make_async_remote_copy(
            src_ref=proj.at[peer], dst_ref=held.at[me],
            send_sem=sems.at[0, step], recv_sem=sems.at[1, step],
            device_id=(ax, peer), device_id_type=MESH))
        copies[-1].start()
    own.wait()
    for copy in copies:
        copy.wait()
    blocks = [held[y].reshape(local_rank * pairs, LANES) for y in range(n_rad)]
    per = LANES // radial
    columns = []
    for y in range(n_rad):
        column = []
        for x in range(n_rad):
            square = dot(blocks[x], blocks[y], 0, 0)
            total = square[:radial, :radial]
            for e in range(1, per):
                total = total + square[e * radial:(e + 1) * radial, e * radial:(e + 1) * radial]
            column.append(total)
        columns.append(jnp.concatenate(column, axis=0))
    size = n_rad * radial
    for c in range(size // LANES):
        part[c * size:(c + 1) * size] = jnp.concatenate(columns[c * per:(c + 1) * per], axis=1)
    groups.all_sum(rows, part, out, *scratch)


def rad_kernel(radial, packed, start, held, factor, core):
    n_rad, local_rank, pairs, _ = held.shape
    size, rank = start.shape
    gram = jnp.concatenate(
        [packed[c * size:(c + 1) * size, :] for c in range(size // LANES)], axis=1
    )
    basis = iterate(gram, start[...]).T
    factor[...] = basis
    per = LANES // radial
    total = None
    for y in range(n_rad):
        own = basis[y * radial:(y + 1) * radial]
        zero = jnp.zeros_like(own)
        spread = jnp.concatenate([
            jnp.concatenate([own if e == f else zero for e in range(per)], axis=0)
            for f in range(per)
        ], axis=1)
        term = dot(held[y].reshape(local_rank * pairs, LANES), spread, 1, 0)
        total = term if total is None else total + term
    for e in range(per):
        core[e * pairs:(e + 1) * pairs, :] = jnp.concatenate([
            total[k * pairs:(k + 1) * pairs, e * rank:(e + 1) * rank] for k in range(local_rank)
        ], axis=1)


def shards(n_ax, n_rad, field, start_az, start_rad):
    snaps, axial, radial, azim = field.shape
    rank = start_az.shape[1]
    cells = snaps * axial
    pairs = cells * radial // LANES
    local_rank = rank // n_rad
    size = n_rad * radial
    groups = Groups(n_ax, n_rad, 4)
    in_vmem = pl.BlockSpec(memory_space=pltpu.VMEM)

    def call(kernel, shapes, scratch, name, collective=None):
        extra = {} if collective is None else dict(collective_id=collective, has_side_effects=True)
        return pl.pallas_call(
            kernel,
            name=name,
            out_shape=[jax.ShapeDtypeStruct(shape, F32) for shape in shapes],
            out_specs=[in_vmem] * len(shapes),
            scratch_shapes=scratch,
            compiler_params=pltpu.CompilerParams(vmem_limit_bytes=VMEM_LIMIT, **extra),
        )

    rows = groups.rows(3 * azim // 2)
    total = groups.near * rows
    (gram_az,) = call(
        functools.partial(gram_az_kernel, groups, rows, 512),
        [(total, LANES)],
        [pltpu.VMEM((total, LANES), F32)] + groups.scratch(rows),
        "gram_az", 0,
    )(field.reshape(-1, azim))
    az_factor, proj = call(
        functools.partial(az_kernel, 8),
        [(azim, rank), (rank, pairs, LANES)], [], "az_factor",
    )(field.reshape(cells, radial, azim), gram_az, start_az)
    rows = groups.rows(size * size // LANES)
    total = groups.near * rows
    shape = (n_rad, local_rank, pairs, LANES)
    gram_rad, held = call(
        functools.partial(gram_rad_kernel, groups, rows, radial),
        [(total, LANES), shape],
        [pltpu.VMEM((total, LANES), F32), pltpu.SemaphoreType.DMA((2, n_rad)),
         pltpu.SemaphoreType.DMA] + groups.scratch(rows),
        "gram_rad", 1,
    )(proj.reshape(shape))
    rad_factor, core = call(
        functools.partial(rad_kernel, radial),
        [(size, rank), (cells, local_rank * rank)], [], "rad_factor",
    )(gram_rad, start_rad, held)
    return core.reshape(snaps, axial, -1), az_factor, rad_factor


def solution(mesh):
    return jax.shard_map(
        functools.partial(shards, mesh.shape["ax"], mesh.shape["rad"]),
        mesh=mesh,
        in_specs=(P(None, "ax", "rad", None), P(), P()),
        out_specs=(P(None, "ax", "rad"), P(), P()),
        check_vma=False,
    )
```

```python
import functools

import jax
import jax.numpy as jnp
from jax import lax
from jax.experimental import pallas as pl
from jax.experimental.pallas import tpu as pltpu
from jax.sharding import PartitionSpec as P

ITERS = 3
LANES = 128
PANEL = 8
CHUNK = 8
GROUP = 8
HIGH = lax.Precision.HIGHEST
MESH = pl.DeviceIdType.MESH
F32 = jnp.float32
BF16 = jnp.bfloat16
VMEM_LIMIT = 48 * 1024 * 1024


def dot(a, b, ca, cb, precision=HIGH):
    return lax.dot_general(
        a, b, (((ca,), (cb,)), ((), ())), precision=precision, preferred_element_type=F32
    )


def dot16(a, b, ca, cb):
    return dot(a, b, ca, cb, lax.Precision.DEFAULT)


def split(value):
    high = value.astype(BF16)
    return high, (value - high.astype(F32)).astype(BF16)


class Groups:
    def __init__(self, n_ax, n_rad, low):
        self.low = min(low, n_ax)
        self.n_rad = n_rad
        self.near = self.low * n_rad
        self.far = n_ax // self.low

    def place(self):
        ax, rad = lax.axis_index("ax"), lax.axis_index("rad")
        return lax.rem(ax, self.low) * self.n_rad + rad, lax.div(ax, self.low)

    def device(self, near, far):
        return (far * self.low + lax.div(near, self.n_rad), lax.rem(near, self.n_rad))

    def rows(self, total):
        return -(-total // (self.near * 8)) * 8

    def greet(self):
        near, far = self.place()
        barrier = pltpu.get_barrier_semaphore()
        for step in range(1, self.near):
            peer = lax.rem(near + step, self.near)
            pl.semaphore_signal(barrier, inc=1, device_id=self.device(peer, far), device_id_type=MESH)
        for step in range(1, self.far):
            peer = lax.rem(far + step, self.far)
            pl.semaphore_signal(barrier, inc=1, device_id=self.device(near, peer), device_id_type=MESH)

    def meet(self):
        pl.semaphore_wait(pltpu.get_barrier_semaphore(), self.near + self.far - 2)

    def scratch(self, rows):
        return [
            pltpu.VMEM((self.near, rows, LANES), F32),
            pltpu.VMEM((self.far, rows, LANES), F32),
            pltpu.SemaphoreType.DMA((2, self.near)),
            pltpu.SemaphoreType.DMA((2, self.far)),
            pltpu.SemaphoreType.DMA((2, self.near)),
        ]

    def all_sum(self, rows, part, out, terms, pieces, sem_a, sem_b, sem_c):
        near, far = self.place()

        def mine(index):
            return pl.ds(pl.multiple_of(index * rows, 8), rows)

        sent = []
        for step in range(1, self.near):
            peer = lax.rem(near + step, self.near)
            sent.append(pltpu.make_async_remote_copy(
                src_ref=part.at[mine(peer)], dst_ref=terms.at[step],
                send_sem=sem_a.at[0, step], recv_sem=sem_a.at[1, step],
                device_id=self.device(peer, far), device_id_type=MESH))
            sent[-1].start()
        total = part[mine(near), :]
        for step in range(1, self.near):
            sent[step - 1].wait_recv()
            total = total + terms[step]
        pieces[far] = total
        for step in range(1, self.far):
            peer = lax.rem(far + step, self.far)
            sent.append(pltpu.make_async_remote_copy(
                src_ref=pieces.at[far], dst_ref=pieces.at[far],
                send_sem=sem_b.at[0, step], recv_sem=sem_b.at[1, step],
                device_id=self.device(near, peer), device_id_type=MESH))
            sent[-1].start()
        for copy in sent[self.near - 1:]:
            copy.wait_recv()
        total = pieces[0]
        for index in range(1, self.far):
            total = total + pieces[index]
        out[mine(near), :] = total
        last = []
        for step in range(1, self.near):
            peer = lax.rem(near + step, self.near)
            last.append(pltpu.make_async_remote_copy(
                src_ref=out.at[mine(near)], dst_ref=out.at[mine(near)],
                send_sem=sem_c.at[0, step], recv_sem=sem_c.at[1, step],
                device_id=self.device(peer, far), device_id_type=MESH))
            last[-1].start()
        for copy in last:
            copy.wait_recv()
        return sent + last


def orthonormal(block):
    rank = block.shape[0]
    inner = dot(block, block, 1, 1)
    index = lax.broadcasted_iota(jnp.int32, (rank, LANES), 0)
    done = []
    for start in range(0, rank, PANEL):
        columns = [
            jnp.broadcast_to(inner[:, start + i:start + i + 1], (rank, LANES)) for i in range(PANEL)
        ]
        for i in range(PANEL):
            k = start + i
            pivot = columns[i][k:k + 1, :]
            inv = lax.rsqrt(pivot)
            inv = inv * (1.5 - 0.5 * pivot * inv * inv)
            lower = jnp.where(index > k, columns[i] * inv, 0.0)
            for j in range(i + 1, PANEL):
                columns[j] = columns[j] - lower * lower[start + j:start + j + 1, :]
            wide = jnp.concatenate([inv] * (block.shape[1] // LANES), axis=1)
            row = block[k:k + 1, :] * wide
            done.append(row)
            spread = jnp.concatenate([lower] * (block.shape[1] // LANES), axis=1)
            block = block - spread * row
            inner = inner - lower[:, :rank] * (inner[k:k + 1, :] * inv[:, :rank])
    return jnp.concatenate(done, axis=0)


def iterate(gram, block):
    for _ in range(ITERS):
        block = orthonormal(dot(block, gram, 1, 0))
    return block


def gram_kernel(groups, rows_az, rows_rad, chunk, group, field, start, factor, out, held,
                cells_ref, loaded, part_az, packed, proj, part_rad, swap_sems, *scratch):
    groups.greet()
    cells, radial, azim = field.shape
    n_rad, local_rank, pairs, _ = held.shape
    rank = start.shape[0]
    half = azim // 2
    ax, me = lax.axis_index("ax"), lax.axis_index("rad")

    def load(step):
        where = pl.ds(step * chunk, chunk)
        return pltpu.make_async_copy(field.at[where], cells_ref.at[where], loaded.at[step])

    for step in range(cells // chunk):
        load(step).start()

    def add(step, total):
        load(step).wait()
        high, low = split(cells_ref[pl.ds(step * chunk, chunk)].reshape(chunk * radial, azim))
        return total + dot16(high, jnp.concatenate([high, low], axis=1), 0, 0)

    total = lax.fori_loop(0, cells // chunk, add, jnp.zeros((azim, 2 * azim), F32))
    mixed = total[:, azim:]
    gram = total[:, :azim] + mixed + mixed.T
    part_az[0:half] = gram[:half, :half]
    part_az[half:2 * half] = gram[:half, half:]
    part_az[2 * half:3 * half] = gram[half:, half:]
    if part_az.shape[0] > 3 * half:
        part_az[3 * half:] = jnp.zeros((part_az.shape[0] - 3 * half, LANES), F32)
    groups.meet()
    sent = groups.all_sum(rows_az, part_az, packed, *scratch[:5])

    cross = packed[half:2 * half, :]
    gram = jnp.concatenate([
        jnp.concatenate([packed[0:half, :], cross], axis=1),
        jnp.concatenate([cross.T, packed[2 * half:3 * half, :]], axis=1),
    ], axis=0)
    block = iterate(gram, start[...])
    factor[...] = block

    high, low = split(block)
    both = jnp.concatenate([high, low], axis=0)
    width = LANES // radial
    swaps = []
    for index in range(pairs // group):
        first = index * group
        here = slice(first, first + group)
        part = jnp.concatenate([
            cells_ref[e * pairs + first:e * pairs + first + group] for e in range(width)
        ], axis=1).reshape(group * LANES, azim)
        f_high, f_low = split(part)
        twice = dot16(both, f_high, 1, 1)
        values = twice[:rank] + twice[rank:] + dot16(high, f_low, 1, 1)
        values = jnp.stack([values[:, i * LANES:(i + 1) * LANES] for i in range(group)], axis=1)
        for y in range(n_rad):
            proj[y, :, here, :] = values[y * local_rank:(y + 1) * local_rank]
        swaps.append([])
        for step in range(1, n_rad):
            peer = lax.rem(me + step, n_rad)
            copy = pltpu.make_async_remote_copy(
                src_ref=proj.at[peer, :, pl.ds(first, group), :],
                dst_ref=held.at[me, :, pl.ds(first, group), :],
                send_sem=swap_sems.at[0, index, step], recv_sem=swap_sems.at[1, index, step],
                device_id=(ax, peer), device_id_type=MESH)
            copy.start()
            swaps[-1].append(copy)
    held[me] = proj[me]

    square = None
    for index in range(pairs // group):
        here = slice(index * group, (index + 1) * group)
        for copy in swaps[index]:
            copy.wait_recv()
        high, low = split(jnp.concatenate([
            held[y, :, here, :].reshape(local_rank * group, LANES) for y in range(n_rad)
        ], axis=1))
        term = dot16(jnp.concatenate([high, low, high], axis=0),
                     jnp.concatenate([high, high, low], axis=0), 0, 0)
        square = term if square is None else square + term
    columns = []
    for y in range(n_rad):
        column = []
        for x in range(n_rad):
            terms = [
                square[x * LANES + e * radial:x * LANES + (e + 1) * radial,
                       y * LANES + e * radial:y * LANES + (e + 1) * radial]
                for e in range(width)
            ]
            column.append(functools.reduce(jnp.add, terms))
        columns.append(jnp.concatenate(column, axis=0))
    size = n_rad * radial
    for c in range(size // LANES):
        part_rad[c * size:(c + 1) * size] = jnp.concatenate(
            columns[c * width:(c + 1) * width], axis=1)
    used = size * size // LANES
    if part_rad.shape[0] > used:
        part_rad[used:] = jnp.zeros((part_rad.shape[0] - used, LANES), F32)
    sent += groups.all_sum(rows_rad, part_rad, out, *scratch[5:])
    for copies in swaps:
        sent += copies
    for copy in sent:
        copy.wait_send()


def rad_kernel(radial, packed, start, held, az_in, az_factor, factor, core):
    n_rad, local_rank, pairs, _ = held.shape
    rank, size = start.shape
    az_factor[...] = az_in[...]
    gram = jnp.concatenate(
        [packed[c * size:(c + 1) * size, :] for c in range(size // LANES)], axis=1
    )
    block = iterate(gram, start[...])
    factor[...] = block
    basis = block.T
    per = LANES // radial
    total = None
    for y in range(n_rad):
        own = basis[y * radial:(y + 1) * radial]
        zero = jnp.zeros_like(own)
        spread = jnp.concatenate([
            jnp.concatenate([own if e == f else zero for e in range(per)], axis=0)
            for f in range(per)
        ], axis=1)
        term = dot(held[y].reshape(local_rank * pairs, LANES), spread, 1, 0)
        total = term if total is None else total + term
    for e in range(per):
        core[e * pairs:(e + 1) * pairs, :] = jnp.concatenate([
            total[k * pairs:(k + 1) * pairs, e * rank:(e + 1) * rank] for k in range(local_rank)
        ], axis=1)


def shards(n_ax, n_rad, field, start_az, start_rad):
    snaps, axial, radial, azim = field.shape
    rank = start_az.shape[1]
    cells = snaps * axial
    pairs = cells * radial // LANES
    local_rank = rank // n_rad
    size = n_rad * radial
    groups = Groups(n_ax, n_rad, 4)
    in_vmem = pl.BlockSpec(memory_space=pltpu.VMEM)
    in_hbm = pl.BlockSpec(memory_space=pltpu.HBM)

    def call(kernel, in_specs, shapes, scratch, name, **extra):
        return pl.pallas_call(
            kernel,
            name=name,
            in_specs=in_specs,
            out_shape=[jax.ShapeDtypeStruct(shape, F32) for shape in shapes],
            out_specs=[in_vmem] * len(shapes),
            scratch_shapes=scratch,
            compiler_params=pltpu.CompilerParams(vmem_limit_bytes=VMEM_LIMIT, **extra),
        )

    rows_az = groups.rows(3 * azim // 2)
    rows_rad = groups.rows(size * size // LANES)
    total_az, total_rad = groups.near * rows_az, groups.near * rows_rad
    shape = (n_rad, local_rank, pairs, LANES)
    chunk, group = CHUNK, GROUP
    az_factor, gram_rad, held = call(
        functools.partial(gram_kernel, groups, rows_az, rows_rad, chunk, group),
        [in_hbm, in_vmem],
        [(rank, azim), (total_rad, LANES), shape],
        [
            pltpu.VMEM((cells, radial, azim), F32),
            pltpu.SemaphoreType.DMA((cells // chunk,)),
            pltpu.VMEM((total_az, LANES), F32),
            pltpu.VMEM((total_az, LANES), F32),
            pltpu.VMEM(shape, F32),
            pltpu.VMEM((total_rad, LANES), F32),
            pltpu.SemaphoreType.DMA((2, pairs // group, n_rad)),
        ] + groups.scratch(rows_az) + groups.scratch(rows_rad),
        "grams", collective_id=0, has_side_effects=True,
    )(field.reshape(cells, radial, azim), start_az.T)
    az_factor, rad_factor, core = call(
        functools.partial(rad_kernel, radial),
        [in_vmem] * 4,
        [(rank, azim), (rank, size), (cells, local_rank * rank)],
        [], "rad_factor",
    )(gram_rad, start_rad.T, held, az_factor)
    return core.reshape(snaps, axial, -1), az_factor.T, rad_factor.T


def solution(mesh):
    return jax.shard_map(
        functools.partial(shards, mesh.shape["ax"], mesh.shape["rad"]),
        mesh=mesh,
        in_specs=(P(None, "ax", "rad", None), P(), P()),
        out_specs=(P(None, "ax", "rad"), P(), P()),
        check_vma=False,
    )
```

```python
import functools

import jax
import jax.numpy as jnp
from jax import lax
from jax.experimental import pallas as pl
from jax.experimental.pallas import tpu as pltpu
from jax.sharding import PartitionSpec as P

ITERS = 3
LANES = 128
PANEL = 32
CHUNK = 8
GROUP = 8
HIGH = lax.Precision.HIGHEST
MESH = pl.DeviceIdType.MESH
F32 = jnp.float32
BF16 = jnp.bfloat16
VMEM_LIMIT = 48 * 1024 * 1024


def dot(a, b, ca, cb, precision=HIGH):
    return lax.dot_general(
        a, b, (((ca,), (cb,)), ((), ())), precision=precision, preferred_element_type=F32
    )


def dot16(a, b, ca, cb):
    return dot(a, b, ca, cb, lax.Precision.DEFAULT)


def split(value):
    high = value.astype(BF16)
    return high, (value - high.astype(F32)).astype(BF16)


class Groups:
    def __init__(self, n_ax, n_rad, low):
        self.low = min(low, n_ax)
        self.n_rad = n_rad
        self.near = self.low * n_rad
        self.far = n_ax // self.low

    def place(self):
        ax, rad = lax.axis_index("ax"), lax.axis_index("rad")
        return lax.rem(ax, self.low) * self.n_rad + rad, lax.div(ax, self.low)

    def device(self, near, far):
        return (far * self.low + lax.div(near, self.n_rad), lax.rem(near, self.n_rad))

    def rows(self, total):
        return -(-total // (self.near * 8)) * 8

    def greet(self):
        near, far = self.place()
        barrier = pltpu.get_barrier_semaphore()
        for step in range(1, self.near):
            peer = lax.rem(near + step, self.near)
            pl.semaphore_signal(barrier, inc=1, device_id=self.device(peer, far), device_id_type=MESH)
        for step in range(1, self.far):
            peer = lax.rem(far + step, self.far)
            pl.semaphore_signal(barrier, inc=1, device_id=self.device(near, peer), device_id_type=MESH)

    def meet(self):
        pl.semaphore_wait(pltpu.get_barrier_semaphore(), self.near + self.far - 2)

    def scratch(self, rows):
        return [
            pltpu.VMEM((self.near, rows, LANES), F32),
            pltpu.VMEM((self.far, rows, LANES), F32),
            pltpu.SemaphoreType.DMA((2, self.near)),
            pltpu.SemaphoreType.DMA((2, self.far)),
            pltpu.SemaphoreType.DMA((2, self.near)),
        ]

    def all_sum(self, rows, part, out, terms, pieces, sem_a, sem_b, sem_c):
        near, far = self.place()

        def mine(index):
            return pl.ds(pl.multiple_of(index * rows, 8), rows)

        sent = []
        for step in range(1, self.near):
            peer = lax.rem(near + step, self.near)
            sent.append(pltpu.make_async_remote_copy(
                src_ref=part.at[mine(peer)], dst_ref=terms.at[step],
                send_sem=sem_a.at[0, step], recv_sem=sem_a.at[1, step],
                device_id=self.device(peer, far), device_id_type=MESH))
            sent[-1].start()
        total = part[mine(near), :]
        for step in range(1, self.near):
            sent[step - 1].wait_recv()
            total = total + terms[step]
        pieces[far] = total
        for step in range(1, self.far):
            peer = lax.rem(far + step, self.far)
            sent.append(pltpu.make_async_remote_copy(
                src_ref=pieces.at[far], dst_ref=pieces.at[far],
                send_sem=sem_b.at[0, step], recv_sem=sem_b.at[1, step],
                device_id=self.device(near, peer), device_id_type=MESH))
            sent[-1].start()
        for copy in sent[self.near - 1:]:
            copy.wait_recv()
        total = pieces[0]
        for index in range(1, self.far):
            total = total + pieces[index]
        out[mine(near), :] = total
        last = []
        for step in range(1, self.near):
            peer = lax.rem(near + step, self.near)
            last.append(pltpu.make_async_remote_copy(
                src_ref=out.at[mine(near)], dst_ref=out.at[mine(near)],
                send_sem=sem_c.at[0, step], recv_sem=sem_c.at[1, step],
                device_id=self.device(peer, far), device_id_type=MESH))
            last[-1].start()
        for copy in last:
            copy.wait_recv()
        return sent + last


def orthonormal(block):
    rank = block.shape[0]
    inner = dot(block, block, 1, 1)
    index = lax.broadcasted_iota(jnp.int32, (rank, LANES), 0)
    done = []
    for start in range(0, rank, PANEL):
        columns = [
            jnp.broadcast_to(inner[:, start + i:start + i + 1], (rank, LANES)) for i in range(PANEL)
        ]
        for i in range(PANEL):
            k = start + i
            pivot = columns[i][k:k + 1, :]
            inv = lax.rsqrt(pivot)
            inv = inv * (1.5 - 0.5 * pivot * inv * inv)
            lower = jnp.where(index > k, columns[i] * inv, 0.0)
            for j in range(i + 1, PANEL):
                columns[j] = columns[j] - lower * lower[start + j:start + j + 1, :]
            wide = jnp.concatenate([inv] * (block.shape[1] // LANES), axis=1)
            row = block[k:k + 1, :] * wide
            done.append(row)
            spread = jnp.concatenate([lower] * (block.shape[1] // LANES), axis=1)
            block = block - spread * row
            inner = inner - lower[:, :rank] * (inner[k:k + 1, :] * inv[:, :rank])
    return jnp.concatenate(done, axis=0)


def iterate(gram, block):
    gram_high, gram_low = split(gram)
    rank = block.shape[0]
    for _ in range(ITERS):
        high, low = split(block)
        twice = dot16(jnp.concatenate([high, low], axis=0), gram_high, 1, 0)
        block = orthonormal(twice[:rank] + twice[rank:] + dot16(high, gram_low, 1, 0))
    return block


def gram_kernel(groups, rows_az, rows_rad, chunk, group, field, start, factor, out, held,
                part_az, packed, proj, part_rad, swap_sems, *scratch):
    groups.greet()
    cells, radial, azim = field.shape
    n_rad, local_rank, pairs, _ = held.shape
    rank = start.shape[0]
    half = azim // 2
    ax, me = lax.axis_index("ax"), lax.axis_index("rad")

    def add(step, total):
        high, low = split(field[pl.ds(step * chunk, chunk)].reshape(chunk * radial, azim))
        return total + dot16(high, jnp.concatenate([high, low], axis=1), 0, 0)

    total = lax.fori_loop(0, cells // chunk, add, jnp.zeros((azim, 2 * azim), F32))
    mixed = total[:, azim:]
    gram = total[:, :azim] + mixed + mixed.T
    part_az[0:half] = gram[:half, :half]
    part_az[half:2 * half] = gram[:half, half:]
    part_az[2 * half:3 * half] = gram[half:, half:]
    if part_az.shape[0] > 3 * half:
        part_az[3 * half:] = jnp.zeros((part_az.shape[0] - 3 * half, LANES), F32)
    groups.meet()
    sent = groups.all_sum(rows_az, part_az, packed, *scratch[:5])

    cross = packed[half:2 * half, :]
    gram = jnp.concatenate([
        jnp.concatenate([packed[0:half, :], cross], axis=1),
        jnp.concatenate([cross.T, packed[2 * half:3 * half, :]], axis=1),
    ], axis=0)
    block = iterate(gram, start[...])
    factor[...] = block

    high, low = split(block)
    both = jnp.concatenate([high, low], axis=0)
    width = LANES // radial
    swaps = []
    for index in range(pairs // group):
        first = index * group
        here = slice(first, first + group)
        part = jnp.concatenate([
            field[e * pairs + first:e * pairs + first + group] for e in range(width)
        ], axis=1).reshape(group * LANES, azim)
        f_high, f_low = split(part)
        twice = dot16(both, f_high, 1, 1)
        values = twice[:rank] + twice[rank:] + dot16(high, f_low, 1, 1)
        values = jnp.stack([values[:, i * LANES:(i + 1) * LANES] for i in range(group)], axis=1)
        for y in range(n_rad):
            proj[y, :, here, :] = values[y * local_rank:(y + 1) * local_rank]
        swaps.append([])
        for step in range(1, n_rad):
            peer = lax.rem(me + step, n_rad)
            copy = pltpu.make_async_remote_copy(
                src_ref=proj.at[peer, :, pl.ds(first, group), :],
                dst_ref=held.at[me, :, pl.ds(first, group), :],
                send_sem=swap_sems.at[0, index, step], recv_sem=swap_sems.at[1, index, step],
                device_id=(ax, peer), device_id_type=MESH)
            copy.start()
            swaps[-1].append(copy)
    held[me] = proj[me]

    square = None
    for index in range(pairs // group):
        here = slice(index * group, (index + 1) * group)
        for copy in swaps[index]:
            copy.wait_recv()
        high, low = split(jnp.concatenate([
            held[y, :, here, :].reshape(local_rank * group, LANES) for y in range(n_rad)
        ], axis=1))
        term = dot16(jnp.concatenate([high, low, high], axis=0),
                     jnp.concatenate([high, high, low], axis=0), 0, 0)
        square = term if square is None else square + term
    columns = []
    for y in range(n_rad):
        column = []
        for x in range(n_rad):
            terms = [
                square[x * LANES + e * radial:x * LANES + (e + 1) * radial,
                       y * LANES + e * radial:y * LANES + (e + 1) * radial]
                for e in range(width)
            ]
            column.append(functools.reduce(jnp.add, terms))
        columns.append(jnp.concatenate(column, axis=0))
    size = n_rad * radial
    for c in range(size // LANES):
        part_rad[c * size:(c + 1) * size] = jnp.concatenate(
            columns[c * width:(c + 1) * width], axis=1)
    used = size * size // LANES
    if part_rad.shape[0] > used:
        part_rad[used:] = jnp.zeros((part_rad.shape[0] - used, LANES), F32)
    sent += groups.all_sum(rows_rad, part_rad, out, *scratch[5:])
    for copies in swaps:
        sent += copies
    for copy in sent:
        copy.wait_send()


def rad_kernel(radial, packed, start, held, az_in, az_factor, factor, core):
    n_rad, local_rank, pairs, _ = held.shape
    rank, size = start.shape
    az_factor[...] = az_in[...]
    gram = jnp.concatenate(
        [packed[c * size:(c + 1) * size, :] for c in range(size // LANES)], axis=1
    )
    block = iterate(gram, start[...])
    factor[...] = block
    basis = block.T
    per = LANES // radial
    total = None
    for y in range(n_rad):
        own = basis[y * radial:(y + 1) * radial]
        zero = jnp.zeros_like(own)
        spread = jnp.concatenate([
            jnp.concatenate([own if e == f else zero for e in range(per)], axis=0)
            for f in range(per)
        ], axis=1)
        term = dot(held[y].reshape(local_rank * pairs, LANES), spread, 1, 0)
        total = term if total is None else total + term
    for e in range(per):
        core[e * pairs:(e + 1) * pairs, :] = jnp.concatenate([
            total[k * pairs:(k + 1) * pairs, e * rank:(e + 1) * rank] for k in range(local_rank)
        ], axis=1)


def shards(n_ax, n_rad, field, start_az, start_rad):
    snaps, axial, radial, azim = field.shape
    rank = start_az.shape[1]
    cells = snaps * axial
    pairs = cells * radial // LANES
    local_rank = rank // n_rad
    size = n_rad * radial
    groups = Groups(n_ax, n_rad, 4)
    in_vmem = pl.BlockSpec(memory_space=pltpu.VMEM)

    def call(kernel, in_specs, shapes, scratch, name, **extra):
        return pl.pallas_call(
            kernel,
            name=name,
            in_specs=in_specs,
            out_shape=[jax.ShapeDtypeStruct(shape, F32) for shape in shapes],
            out_specs=[in_vmem] * len(shapes),
            scratch_shapes=scratch,
            compiler_params=pltpu.CompilerParams(vmem_limit_bytes=VMEM_LIMIT, **extra),
        )

    rows_az = groups.rows(3 * azim // 2)
    rows_rad = groups.rows(size * size // LANES)
    total_az, total_rad = groups.near * rows_az, groups.near * rows_rad
    shape = (n_rad, local_rank, pairs, LANES)
    chunk, group = CHUNK, GROUP
    az_factor, gram_rad, held = call(
        functools.partial(gram_kernel, groups, rows_az, rows_rad, chunk, group),
        [in_vmem, in_vmem],
        [(rank, azim), (total_rad, LANES), shape],
        [
            pltpu.VMEM((total_az, LANES), F32),
            pltpu.VMEM((total_az, LANES), F32),
            pltpu.VMEM(shape, F32),
            pltpu.VMEM((total_rad, LANES), F32),
            pltpu.SemaphoreType.DMA((2, pairs // group, n_rad)),
        ] + groups.scratch(rows_az) + groups.scratch(rows_rad),
        "grams", collective_id=0, has_side_effects=True,
    )(field.reshape(cells, radial, azim), start_az.T)
    az_factor, rad_factor, core = call(
        functools.partial(rad_kernel, radial),
        [in_vmem] * 4,
        [(rank, azim), (rank, size), (cells, local_rank * rank)],
        [], "rad_factor",
    )(gram_rad, start_rad.T, held, az_factor)
    return core.reshape(snaps, axial, -1), az_factor.T, rad_factor.T


def solution(mesh):
    return jax.shard_map(
        functools.partial(shards, mesh.shape["ax"], mesh.shape["rad"]),
        mesh=mesh,
        in_specs=(P(None, "ax", "rad", None), P(), P()),
        out_specs=(P(None, "ax", "rad"), P(), P()),
        check_vma=False,
    )
```

```python
import functools

import jax
import jax.numpy as jnp
from jax import lax
from jax.experimental import pallas as pl
from jax.experimental.pallas import tpu as pltpu
from jax.sharding import PartitionSpec as P

ITERS = 3
LANES = 128
PANEL = 32
CHUNK = 32
GROUP = 8
HIGH = lax.Precision.HIGHEST
MESH = pl.DeviceIdType.MESH
F32 = jnp.float32
BF16 = jnp.bfloat16
VMEM_LIMIT = 48 * 1024 * 1024


def dot(a, b, ca, cb, precision=HIGH):
    return lax.dot_general(
        a, b, (((ca,), (cb,)), ((), ())), precision=precision, preferred_element_type=F32
    )


def dot16(a, b, ca, cb):
    return dot(a, b, ca, cb, lax.Precision.DEFAULT)


def split(value):
    high = value.astype(BF16)
    return high, (value - high.astype(F32)).astype(BF16)


def dot3(a, b):
    a_high, a_low = split(a)
    b_high, b_low = split(b)
    return dot16(jnp.concatenate([a_high, a_low], axis=1), jnp.concatenate([b_high, b_high], axis=0), 1, 0) + dot16(a_high, b_low, 1, 0)


class Groups:
    def __init__(self, n_ax, n_rad, low):
        self.low = min(low, n_ax)
        self.n_rad = n_rad
        self.near = self.low * n_rad
        self.far = n_ax // self.low

    def place(self):
        ax, rad = lax.axis_index("ax"), lax.axis_index("rad")
        return lax.rem(ax, self.low) * self.n_rad + rad, lax.div(ax, self.low)

    def device(self, near, far):
        return (far * self.low + lax.div(near, self.n_rad), lax.rem(near, self.n_rad))

    def rows(self, total):
        return -(-total // (self.near * 8)) * 8

    def greet(self):
        near, far = self.place()
        barrier = pltpu.get_barrier_semaphore()
        for step in range(1, self.near):
            peer = lax.rem(near + step, self.near)
            pl.semaphore_signal(barrier, inc=1, device_id=self.device(peer, far), device_id_type=MESH)
        for step in range(1, self.far):
            peer = lax.rem(far + step, self.far)
            pl.semaphore_signal(barrier, inc=1, device_id=self.device(near, peer), device_id_type=MESH)

    def meet(self):
        pl.semaphore_wait(pltpu.get_barrier_semaphore(), self.near + self.far - 2)

    def scratch(self, rows):
        return [
            pltpu.VMEM((self.near, rows, LANES), F32),
            pltpu.VMEM((self.far, rows, LANES), F32),
            pltpu.SemaphoreType.DMA((2, self.near)),
            pltpu.SemaphoreType.DMA((2, self.far)),
            pltpu.SemaphoreType.DMA((2, self.near)),
        ]

    def all_sum(self, rows, part, out, terms, pieces, sem_a, sem_b, sem_c):
        near, far = self.place()

        def mine(index):
            return pl.ds(pl.multiple_of(index * rows, 8), rows)

        sent = []
        for step in range(1, self.near):
            peer = lax.rem(near + step, self.near)
            sent.append(pltpu.make_async_remote_copy(
                src_ref=part.at[mine(peer)], dst_ref=terms.at[step],
                send_sem=sem_a.at[0, step], recv_sem=sem_a.at[1, step],
                device_id=self.device(peer, far), device_id_type=MESH))
            sent[-1].start()
        total = part[mine(near), :]
        for step in range(1, self.near):
            sent[step - 1].wait_recv()
            total = total + terms[step]
        pieces[far] = total
        for step in range(1, self.far):
            peer = lax.rem(far + step, self.far)
            sent.append(pltpu.make_async_remote_copy(
                src_ref=pieces.at[far], dst_ref=pieces.at[far],
                send_sem=sem_b.at[0, step], recv_sem=sem_b.at[1, step],
                device_id=self.device(near, peer), device_id_type=MESH))
            sent[-1].start()
        for copy in sent[self.near - 1:]:
            copy.wait_recv()
        total = pieces[0]
        for index in range(1, self.far):
            total = total + pieces[index]
        out[mine(near), :] = total
        last = []
        for step in range(1, self.near):
            peer = lax.rem(near + step, self.near)
            last.append(pltpu.make_async_remote_copy(
                src_ref=out.at[mine(near)], dst_ref=out.at[mine(near)],
                send_sem=sem_c.at[0, step], recv_sem=sem_c.at[1, step],
                device_id=self.device(peer, far), device_id_type=MESH))
            last[-1].start()
        for copy in last:
            copy.wait_recv()
        return sent + last


def orthonormal(block):
    rank = block.shape[0]
    inner = dot(block, block, 1, 1)
    index = lax.broadcasted_iota(jnp.int32, (rank, LANES), 0)
    done = []
    for start in range(0, rank, PANEL):
        columns = [
            jnp.broadcast_to(inner[:, start + i:start + i + 1], (rank, LANES)) for i in range(PANEL)
        ]
        for i in range(PANEL):
            k = start + i
            pivot = columns[i][k:k + 1, :]
            inv = lax.rsqrt(pivot)
            inv = inv * (1.5 - 0.5 * pivot * inv * inv)
            lower = jnp.where(index > k, columns[i] * inv, 0.0)
            for j in range(i + 1, PANEL):
                columns[j] = columns[j] - lower * lower[start + j:start + j + 1, :]
            wide = jnp.concatenate([inv] * (block.shape[1] // LANES), axis=1)
            row = block[k:k + 1, :] * wide
            done.append(row)
            spread = jnp.concatenate([lower] * (block.shape[1] // LANES), axis=1)
            block = block - spread * row
            inner = inner - lower[:, :rank] * (inner[k:k + 1, :] * inv[:, :rank])
    return jnp.concatenate(done, axis=0)


def iterate(gram, block):
    gram_high, gram_low = split(gram)
    rank = block.shape[0]
    for _ in range(ITERS):
        high, low = split(block)
        twice = dot16(jnp.concatenate([high, low], axis=0), gram_high, 1, 0)
        block = orthonormal(twice[:rank] + twice[rank:] + dot16(high, gram_low, 1, 0))
    return block


def gram_kernel(groups, rows_az, rows_rad, chunk, group, field, start, factor, out, held,
                part_az, packed, proj, part_rad, swap_sems, *scratch):
    groups.greet()
    cells, radial, azim = field.shape
    n_rad, local_rank, pairs, _ = held.shape
    rank = start.shape[0]
    half = azim // 2
    ax, me = lax.axis_index("ax"), lax.axis_index("rad")

    def add(step, total):
        high, low = split(field[pl.ds(step * chunk, chunk)].reshape(chunk * radial, azim))
        return total + dot16(high, jnp.concatenate([high, low], axis=1), 0, 0)

    total = lax.fori_loop(0, cells // chunk, add, jnp.zeros((azim, 2 * azim), F32))
    mixed = total[:, azim:]
    gram = total[:, :azim] + mixed + mixed.T
    part_az[0:half] = gram[:half, :half]
    part_az[half:2 * half] = gram[:half, half:]
    part_az[2 * half:3 * half] = gram[half:, half:]
    if part_az.shape[0] > 3 * half:
        part_az[3 * half:] = jnp.zeros((part_az.shape[0] - 3 * half, LANES), F32)
    groups.meet()
    sent = groups.all_sum(rows_az, part_az, packed, *scratch[:5])

    cross = packed[half:2 * half, :]
    gram = jnp.concatenate([
        jnp.concatenate([packed[0:half, :], cross], axis=1),
        jnp.concatenate([cross.T, packed[2 * half:3 * half, :]], axis=1),
    ], axis=0)
    block = iterate(gram, start[...])
    factor[...] = block

    high, low = split(block)
    both = jnp.concatenate([high, low], axis=0)
    width = LANES // radial
    swaps = []
    for index in range(pairs // group):
        first = index * group
        here = slice(first, first + group)
        part = jnp.concatenate([
            field[e * pairs + first:e * pairs + first + group] for e in range(width)
        ], axis=1).reshape(group * LANES, azim)
        f_high, f_low = split(part)
        twice = dot16(both, f_high, 1, 1)
        values = twice[:rank] + twice[rank:] + dot16(high, f_low, 1, 1)
        values = jnp.stack([values[:, i * LANES:(i + 1) * LANES] for i in range(group)], axis=1)
        for y in range(n_rad):
            proj[y, :, here, :] = values[y * local_rank:(y + 1) * local_rank]
        swaps.append([])
        for step in range(1, n_rad):
            peer = lax.rem(me + step, n_rad)
            copy = pltpu.make_async_remote_copy(
                src_ref=proj.at[peer, :, pl.ds(first, group), :],
                dst_ref=held.at[me, :, pl.ds(first, group), :],
                send_sem=swap_sems.at[0, index, step], recv_sem=swap_sems.at[1, index, step],
                device_id=(ax, peer), device_id_type=MESH)
            copy.start()
            swaps[-1].append(copy)
    held[me] = proj[me]

    square = None
    for index in range(pairs // group):
        here = slice(index * group, (index + 1) * group)
        for copy in swaps[index]:
            copy.wait_recv()
        high, low = split(jnp.concatenate([
            held[y, :, here, :].reshape(local_rank * group, LANES) for y in range(n_rad)
        ], axis=1))
        term = dot16(jnp.concatenate([high, low, high], axis=0),
                     jnp.concatenate([high, high, low], axis=0), 0, 0)
        square = term if square is None else square + term
    columns = []
    for y in range(n_rad):
        column = []
        for x in range(n_rad):
            terms = [
                square[x * LANES + e * radial:x * LANES + (e + 1) * radial,
                       y * LANES + e * radial:y * LANES + (e + 1) * radial]
                for e in range(width)
            ]
            column.append(functools.reduce(jnp.add, terms))
        columns.append(jnp.concatenate(column, axis=0))
    size = n_rad * radial
    for c in range(size // LANES):
        part_rad[c * size:(c + 1) * size] = jnp.concatenate(
            columns[c * width:(c + 1) * width], axis=1)
    used = size * size // LANES
    if part_rad.shape[0] > used:
        part_rad[used:] = jnp.zeros((part_rad.shape[0] - used, LANES), F32)
    sent += groups.all_sum(rows_rad, part_rad, out, *scratch[5:])
    for copies in swaps:
        sent += copies
    for copy in sent:
        copy.wait_send()


def rad_kernel(radial, packed, start, held, az_in, az_factor, factor, core):
    n_rad, local_rank, pairs, _ = held.shape
    rank, size = start.shape
    az_factor[...] = az_in[...]
    gram = jnp.concatenate(
        [packed[c * size:(c + 1) * size, :] for c in range(size // LANES)], axis=1
    )
    block = iterate(gram, start[...])
    factor[...] = block
    basis = block.T
    per = LANES // radial
    total = None
    for y in range(n_rad):
        own = basis[y * radial:(y + 1) * radial]
        zero = jnp.zeros_like(own)
        spread = jnp.concatenate([
            jnp.concatenate([own if e == f else zero for e in range(per)], axis=0)
            for f in range(per)
        ], axis=1)
        term = dot3(held[y].reshape(local_rank * pairs, LANES), spread)
        total = term if total is None else total + term
    for e in range(per):
        core[e * pairs:(e + 1) * pairs, :] = jnp.concatenate([
            total[k * pairs:(k + 1) * pairs, e * rank:(e + 1) * rank] for k in range(local_rank)
        ], axis=1)


def shards(n_ax, n_rad, field, start_az, start_rad):
    snaps, axial, radial, azim = field.shape
    rank = start_az.shape[1]
    cells = snaps * axial
    pairs = cells * radial // LANES
    local_rank = rank // n_rad
    size = n_rad * radial
    groups = Groups(n_ax, n_rad, 4)
    in_vmem = pl.BlockSpec(memory_space=pltpu.VMEM)

    def call(kernel, in_specs, shapes, scratch, name, **extra):
        return pl.pallas_call(
            kernel,
            name=name,
            in_specs=in_specs,
            out_shape=[jax.ShapeDtypeStruct(shape, F32) for shape in shapes],
            out_specs=[in_vmem] * len(shapes),
            scratch_shapes=scratch,
            compiler_params=pltpu.CompilerParams(vmem_limit_bytes=VMEM_LIMIT, **extra),
        )

    rows_az = groups.rows(3 * azim // 2)
    rows_rad = groups.rows(size * size // LANES)
    total_az, total_rad = groups.near * rows_az, groups.near * rows_rad
    shape = (n_rad, local_rank, pairs, LANES)
    chunk, group = CHUNK, GROUP
    az_factor, gram_rad, held = call(
        functools.partial(gram_kernel, groups, rows_az, rows_rad, chunk, group),
        [in_vmem, in_vmem],
        [(rank, azim), (total_rad, LANES), shape],
        [
            pltpu.VMEM((total_az, LANES), F32),
            pltpu.VMEM((total_az, LANES), F32),
            pltpu.VMEM(shape, F32),
            pltpu.VMEM((total_rad, LANES), F32),
            pltpu.SemaphoreType.DMA((2, pairs // group, n_rad)),
        ] + groups.scratch(rows_az) + groups.scratch(rows_rad),
        "grams", collective_id=0, has_side_effects=True,
    )(field.reshape(cells, radial, azim), start_az.T)
    az_factor, rad_factor, core = call(
        functools.partial(rad_kernel, radial),
        [in_vmem] * 4,
        [(rank, azim), (rank, size), (cells, local_rank * rank)],
        [], "rad_factor",
    )(gram_rad, start_rad.T, held, az_factor)
    return core.reshape(snaps, axial, -1), az_factor.T, rad_factor.T


def solution(mesh):
    return jax.shard_map(
        functools.partial(shards, mesh.shape["ax"], mesh.shape["rad"]),
        mesh=mesh,
        in_specs=(P(None, "ax", "rad", None), P(), P()),
        out_specs=(P(None, "ax", "rad"), P(), P()),
        check_vma=False,
    )
```
